512 devices in a mesh: seq: 64 (over y, z_lo, core), chan: 8 (over x, z_hi).
Axes of the slice: x: 4, y: 4, z: 16 (z_hi: 2, z_lo: 8; z = z_hi * 8 + z_lo), core: 2. Of those that a mesh axis runs over, the one named last changes fastest.
Arguments:
- queries: bfloat16 [16384, 4096], P('seq', 'chan'), may hold values from -6 to 6
- key_proj: bfloat16 [16384, 4096], P('seq', 'chan'), may hold values from -6 to 6
- value_proj: bfloat16 [16384, 4096], P('seq', 'chan'), may hold values from -6 to 6
- decay_rate: float32 [4096, 16], P('chan'), may hold values from 1 to 546
- residues: float32 [4096, 16], P('chan'), may hold values from -1 to 1
- skip_gain: float32 [4096], P('chan'), may hold values from -1 to 1
- out_weight: bfloat16 [4096, 4096], P('chan'), may hold values from -0.125 to 0.125
Outputs:
- layer_out: bfloat16 [16384, 4096], P('seq', 'chan')
The draws below stay inside these ranges and needn't reach their ends.
All inputs are finite; a program needn't handle non-finite values.
Results may differ from the reference program's by a relative error of at most 0.0049.
Values sent between devices are 32-bit elements; how exact they have to be, the bound alone decides.
No kernel may reach another device: no remote copies, remote signals or barrier semaphores. Data moves between devices by JAX's collectives and lax.ppermute only.
A program may use at most 128 MiB of HBM per device.

```python
import math
import jax
import jax.numpy as jnp
from jax import lax

D = 4096
MODES = 16
L = 16384


def draw_decay_rate(key, part):
    key = jax.random.fold_in(key, 7)
    upper = float(L // 30)
    fraction = jax.random.uniform(key, (D, MODES), jnp.float32)
    return jnp.exp(fraction * math.log(upper))


def with_spikes(array, own_key, source, target, parts, factor):
    owner, partner = [(jnp.arange(array.shape[axis_at]) // (array.shape[axis_at] // parts)).reshape([-1 if axis == axis_at else 1 for axis in range(array.ndim)]) for axis_at in (source, target)]
    chosen = jax.random.permutation(own_key, parts)[partner]
    strong = (owner == chosen) | (owner == (partner + parts // 2) % parts)
    return jnp.where(strong, factor * array, array)


def block_levels(own_key, dims, split, least, top_value):
    loudness, own = 1.0, jax.random.fold_in(own_key, 6)
    for dim, shards_of in split:
        steps = jnp.exp(jax.random.uniform(jax.random.fold_in(own, dim), (shards_of,), jnp.float32, least / len(split), top_value / len(split)))
        loudness = loudness * jnp.repeat(steps, dims[dim] // shards_of).reshape([-1 if axis == dim else 1 for axis in range(len(dims))])
    return loudness


def noise(rng, dims, spread, reach, split=(), kind=jnp.bfloat16):
    level = block_levels(rng, dims, split, -0.22, 0.18) if split else 1.0
    array = jax.random.normal(rng, dims, jnp.float32) * spread * level
    return jnp.minimum(jnp.maximum(array, -reach), reach).astype(kind)


def gaussian_with(key, extent, spread, reach, pieces, heavy, held_as=jnp.bfloat16):
    entries = spread * jax.random.normal(key, extent, jnp.float32)
    if pieces:
        entries = entries * block_levels(key, extent, pieces, -0.22, 0.18)
    return jnp.clip(with_spikes(entries, jax.random.fold_in(key, 3), *heavy), -reach, reach).astype(held_as)


def setup_inputs(seed: int = 0) -> dict:
    splits = jax.random.split(jax.random.key(seed), 8)
    return {
        "queries": noise(splits[0], (L, D), 1.0, 6.0, ((0, 64), (1, 8))),
        "key_proj": noise(splits[1], (L, D), 1.0, 6.0, ((0, 64), (1, 8))),
        "value_proj": noise(splits[2], (L, D), 1.0, 6.0, ((0, 64), (1, 8))),
        "decay_rate": draw_decay_rate(jax.random.fold_in(splits[7], 71), 0),
        "residues": jnp.clip(jax.random.uniform(splits[4], (D, MODES), jnp.float32, -1.0, 1.0) * block_levels(splits[4], (D, MODES), ((0, 8),), -0.4, 0.0), -1.0, 1.0),
        "skip_gain": jnp.clip(jax.random.uniform(splits[5], (D,), jnp.float32, -1.0, 1.0) * block_levels(splits[5], (D,), ((0, 8),), -0.4, 0.0), -1.0, 1.0),
        "out_weight": gaussian_with(splits[6], (D, D), D ** -0.5, 0.125, ((0, 8),), (0, 1, 8, 2.0)),
    }


def build_filter(decay_rate, residues, positions, length):

    def add_mode(mode, totals):
        rate_col = lax.dynamic_slice_in_dim(decay_rate, mode, 1, 1)[:, 0]
        weight_col = lax.dynamic_slice_in_dim(residues, mode, 1, 1)[:, 0]
        coefficient = weight_col * jnp.sqrt(2.0 * rate_col / length)
        return totals + coefficient[None, :] * jnp.exp(-positions[:, None] * (rate_col[None, :] / length))
    start = jnp.zeros((positions.shape[0], decay_rate.shape[0]), jnp.float32)
    return lax.fori_loop(0, decay_rate.shape[1], add_mode, start)

def reference(queries, key_proj, value_proj, decay_rate, residues, skip_gain, out_weight):
    mixed_in = key_proj.astype(jnp.float32) * value_proj.astype(jnp.float32)
    positions = jnp.arange(L).astype(jnp.float32)
    filter_time = build_filter(decay_rate, residues, positions, L)
    spectrum = jnp.fft.rfft(mixed_in, n=2 * L, axis=0) * jnp.fft.rfft(filter_time, n=2 * L, axis=0)
    conv = jnp.fft.irfft(spectrum, n=2 * L, axis=0)[:L]
    gated = (queries.astype(jnp.float32) * (conv + skip_gain[None, :] * mixed_in)).astype(jnp.bfloat16)
    return jnp.dot(gated, out_weight, preferred_element_type=jnp.float32).astype(jnp.bfloat16)
```

```python
import functools

import jax
import jax.numpy as jnp
from jax import lax
from jax.experimental import pallas as pl
from jax.experimental.pallas import tpu as pltpu
from jax.sharding import Mesh
from jax.sharding import PartitionSpec as P

F32 = jnp.float32
LANES = 128
SUBS = 8
ALL_VMEM = 56 * 1024 * 1024
MOST_VMEM = 52 * 1024 * 1024
CHUNKS = 2
SEQ_PARTS = (("y", 4), ("zl", 8), ("core", 2))
CHAN_PARTS = (("x", 4), ("zh", 2))
SEQ = tuple(name for name, _ in SEQ_PARTS)
CHAN = tuple(name for name, _ in CHAN_PARTS)


def tree_sum(terms):
    while len(terms) > 1:
        terms = [a + b for a, b in zip(terms[::2], terms[1::2])]
    return terms[0]


def whole_call(kernel, out_shape, scratch_shapes, vmem, args, in_specs=None):
    return pl.pallas_call(
        kernel,
        in_specs=in_specs or [pl.BlockSpec(memory_space=pltpu.VMEM)] * len(args),
        out_specs=jax.tree.map(lambda _: pl.BlockSpec(memory_space=pltpu.VMEM), out_shape),
        out_shape=out_shape,
        scratch_shapes=scratch_shapes,
        compiler_params=pltpu.CompilerParams(vmem_limit_bytes=vmem),
        cost_estimate=pl.CostEstimate(flops=1 << 24, bytes_accessed=1 << 21, transcendentals=0),
    )(*args)


def mix_into(x_ref, k_ref, v_ref):
    tokens, chans = k_ref.shape
    for tile in range(chans // LANES):
        lanes = pl.ds(tile * LANES, LANES)
        x_ref[pl.ds(tile * tokens, tokens), :] = k_ref[:, lanes].astype(F32) * v_ref[:, lanes].astype(F32)


def spread_row(ref, row, lanes):
    return jnp.broadcast_to(ref[row : row + 1, lanes], (SUBS, LANES))


def state_kernel(length, *refs):
    hbm, refs = refs[:4], refs[4:]
    rate_ref, coef_ref, ends_ref, state_ref, fade_ref, x_ref, *arrived, sems = refs
    copies = [pltpu.make_async_copy(src, dst, sems.at[i]) for i, (src, dst) in enumerate(zip(hbm, arrived))]
    for copy in copies:
        copy.start()
    for copy in copies:
        copy.wait()
    k_ref, v_ref, decay_ref, res_ref = arrived
    tokens, chans = k_ref.shape
    modes = rate_ref.shape[0]
    run = tokens // SUBS
    mix_into(x_ref, k_ref, v_ref)
    rate = decay_ref[...] / length
    rate_ref[...] = rate
    coef_ref[...] = res_ref[...] * jnp.sqrt(2.0 * rate)
    later = (SUBS - 1 - lax.broadcasted_iota(jnp.int32, (SUBS, LANES), 0)).astype(F32) * run
    for tile in range(chans // LANES):
        lanes = pl.ds(tile * LANES, LANES)
        rates = [spread_row(rate_ref, m, lanes) for m in range(modes)]
        steps = [jnp.exp(-r) for r in rates]

        def body(j, held, base=tile * tokens):
            x = x_ref[pl.ds(base + j, SUBS, stride=run), :]
            return tuple(a * h + x for a, h in zip(steps, held))

        held = tuple(jnp.zeros((SUBS, LANES), F32) for _ in range(modes))
        held = lax.fori_loop(0, run, body, held, unroll=8)
        for m in range(modes):
            ends_ref[m, :, lanes] = held[m]
            row = m * (chans // LANES) + tile
            state_ref[row : row + 1, :] = jnp.sum(held[m] * jnp.exp(-rates[m] * later), axis=0, keepdims=True)
            fade_ref[row : row + 1, :] = jnp.exp(-rates[m][:1] * tokens)


def local_kernel(x_ref, rate_ref, coef_ref, ends_ref, skip_ref, out_ref, y_ref):
    chans = rate_ref.shape[1]
    tokens = x_ref.shape[0] * LANES // chans
    modes = rate_ref.shape[0]
    run = tokens // SUBS
    place = lax.broadcasted_iota(jnp.int32, (SUBS, LANES), 0)

    def down(value, by):
        return jnp.where(place >= by, pltpu.roll(value, by, 0), 0.0)

    for tile in range(chans // LANES):
        lanes = pl.ds(tile * LANES, LANES)
        steps, held = [], []
        for m in range(modes):
            rate = spread_row(rate_ref, m, lanes)
            steps.append(jnp.exp(-rate))
            total = ends_ref[m, :, lanes]
            for by in (1, 2, 4):
                total = total + jnp.exp(-rate * (by * run)) * down(total, by)
            held.append(down(total, 1))
        coefs = [spread_row(coef_ref, m, lanes) for m in range(modes)]

        def body(j, held, base=tile * tokens):
            x = x_ref[pl.ds(base + j, SUBS, stride=run), :]
            held = tuple(a * h + x for a, h in zip(steps, held))
            y_ref[pl.ds(base + j, SUBS, stride=run), :] = tree_sum([c * h for c, h in zip(coefs, held)])
            return held

        lax.fori_loop(0, run, body, tuple(held), unroll=4)
        rows = pl.ds(tile * tokens, tokens)
        out_ref[rows, :] = y_ref[rows, :] + skip_ref[:, lanes] * x_ref[rows, :]


def gate_kernel(q_ref, local_ref, rate_ref, coef_ref, enter_ref, out_ref, y_ref):
    tokens, chans = q_ref.shape
    modes = rate_ref.shape[0]
    run = tokens // SUBS
    place = (lax.broadcasted_iota(jnp.int32, (SUBS, LANES), 0) * run + 1).astype(F32)
    for tile in range(chans // LANES):
        lanes = pl.ds(tile * LANES, LANES)
        steps, held = [], []
        for m in range(modes):
            rate = spread_row(rate_ref, m, lanes)
            steps.append(jnp.exp(-rate))
            weight = spread_row(coef_ref, m, lanes) * spread_row(enter_ref, m * (chans // LANES) + tile, slice(None))
            held.append(weight * jnp.exp(-rate * place))

        def body(j, held, base=tile * tokens):
            y_ref[pl.ds(base + j, SUBS, stride=run), :] = tree_sum(list(held))
            return tuple(a * h for a, h in zip(steps, held))

        lax.fori_loop(0, run, body, tuple(held), unroll=4)
        rows = pl.ds(tile * tokens, tokens)
        value = q_ref[:, lanes].astype(F32) * (local_ref[rows, :] + y_ref[rows, :])
        out_ref[:, lanes] = value.astype(out_ref.dtype)


def project_kernel(adds, joined, width, cols_ref, gated_ref, weight_ref, *refs):
    terms, outs, (block_ref, sems) = refs[: len(adds)], refs[len(adds) : -2], refs[-2:]
    fetches = start_fetches(cols_ref, width, weight_ref, block_ref, sems)
    for half in range(2):
        fetches[half].wait()
        block = jnp.dot(gated_ref[...], block_ref[half], preferred_element_type=F32)
        for which, term in zip(adds, terms):
            if which == half:
                block = block + term[...]
        if joined:
            outs[0][half] = block
        else:
            outs[half][...] = block


def own_kernel(width, cols_ref, gated_ref, weight_ref, left_ref, right_ref, keep_ref, send_ref, block_ref, sems):
    fetches = start_fetches(cols_ref, width, weight_ref, block_ref, sems)
    mine = cols_ref[2]
    for half, at, out in ((1, 1 - mine, send_ref), (0, mine, keep_ref)):
        fetches[half].wait()
        block = jnp.dot(gated_ref[...], block_ref[half], preferred_element_type=F32)
        out[...] = block + left_ref[at] + right_ref[at]


def start_fetches(cols_ref, width, weight_ref, block_ref, sems):
    fetches = []
    for half in range(2):
        lanes = pl.ds(pl.multiple_of(cols_ref[half] * width, LANES), width)
        fetches.append(pltpu.make_async_copy(weight_ref.at[:, lanes], block_ref.at[half], sems.at[half]))
        fetches[-1].start()
    return fetches


def project_call(kernel, shapes, width, cols, gated, weight, terms):
    vmem = pl.BlockSpec(memory_space=pltpu.VMEM)
    return pl.pallas_call(
        kernel,
        in_specs=[pl.BlockSpec(memory_space=pltpu.SMEM), vmem, pl.BlockSpec(memory_space=pl.ANY)] + [vmem] * len(terms),
        out_specs=[vmem] * len(shapes),
        out_shape=shapes,
        scratch_shapes=[pltpu.VMEM((2, weight.shape[0], width), weight.dtype), pltpu.SemaphoreType.DMA((2,))],
        compiler_params=pltpu.CompilerParams(vmem_limit_bytes=MOST_VMEM),
        cost_estimate=pl.CostEstimate(flops=1 << 27, bytes_accessed=1 << 20, transcendentals=0),
    )(cols, gated, weight, *terms)


def project(gated, weight, cols, width, adds=(), terms=(), joined=False):
    tokens = gated.shape[0]
    if joined:
        shapes = (jax.ShapeDtypeStruct((2, tokens, width), F32),)
    else:
        shapes = (jax.ShapeDtypeStruct((tokens, width), F32),) * 2
    outs = project_call(functools.partial(project_kernel, adds, joined, width), shapes, width, cols, gated, weight, terms)
    return outs[0] if joined else outs


def project_own(gated, weight, cols, width, z_index, terms):
    cols = jnp.concatenate([cols, z_index.astype(jnp.int32)[None]])
    shapes = (jax.ShapeDtypeStruct((gated.shape[0], width), F32),) * 2
    return project_call(functools.partial(own_kernel, width), shapes, width, cols, gated, weight, terms)


def shift(value, axis, by):
    size = lax.axis_size(axis)
    return lax.ppermute(value, axis, [(i, (i + by) % size) for i in range(size)])


def scan_kernel(state_ref, fade_ref, enter_ref):
    count, total = fade_ref.shape[0], jnp.zeros(fade_ref.shape, F32)
    for first in range(0, state_ref.shape[0], count):
        enter_ref[first : first + count, :] = total
        total = total * fade_ref[...] + state_ref[first : first + count, :]


def entering_states(state, fade):
    count, index = state.shape[0], jnp.int32(0)
    for axis in SEQ:
        count = count // lax.axis_size(axis)
        index = index * lax.axis_size(axis) + lax.axis_index(axis)
    fade = lax.dynamic_slice_in_dim(fade, index * count, count, 0)
    state = lax.all_to_all(state, SEQ, 0, 0, tiled=True)
    enter = whole_call(scan_kernel, jax.ShapeDtypeStruct(state.shape, F32), [], MOST_VMEM, (state, fade))
    return lax.all_to_all(enter, SEQ, 0, 0, tiled=True)


def per_device(queries, key_proj, value_proj, decay_rate, residues, skip_gain, out_weight):
    tokens, chans = queries.shape
    modes = decay_rate.shape[1]
    seq_size = 1
    for axis in SEQ:
        seq_size *= lax.axis_size(axis)
    small = jax.ShapeDtypeStruct((modes, chans), F32)
    stacked = jax.ShapeDtypeStruct((tokens * chans // LANES, LANES), F32)
    args = (key_proj, value_proj, decay_rate.T, residues.T)
    ends = jax.ShapeDtypeStruct((modes, SUBS, chans), F32)
    rows = jax.ShapeDtypeStruct((modes * chans // LANES, LANES), F32)
    rate, coef, ends, state, fade, mixed = whole_call(
        functools.partial(state_kernel, float(tokens * seq_size)),
        (small, small, ends, rows, rows, stacked),
        [pltpu.VMEM(a.shape, a.dtype) for a in args] + [pltpu.SemaphoreType.DMA((len(args),))],
        ALL_VMEM,
        args,
        [pl.BlockSpec(memory_space=pl.ANY)] * len(args),
    )
    scratch = [pltpu.VMEM(stacked.shape, F32)]
    local = whole_call(local_kernel, stacked, scratch, ALL_VMEM, (mixed, rate, coef, ends, skip_gain[None, :]))
    enter = entering_states(state, fade)
    gated = jax.ShapeDtypeStruct((tokens, chans), queries.dtype)
    gated = whole_call(gate_kernel, gated, scratch, ALL_VMEM, (queries, local, rate, coef, enter))

    x_size, x_index = lax.axis_size("x"), lax.axis_index("x")
    z_size, z_index = lax.axis_size("zh"), lax.axis_index("zh")
    features = out_weight.shape[1] // (x_size * z_size)
    width = features // CHUNKS

    def cols(x_by, first, chunk):
        start = ((x_index + x_by) % x_size) * z_size
        return ((start + jnp.stack([first, 1 - first])) * CHUNKS + chunk).astype(jnp.int32)

    zero = jnp.int32(0)
    outs, summed, kept, swapped = [], [], [], []
    for chunk in range(CHUNKS + 2):
        if chunk < CHUNKS:
            behind = summed[chunk - 2 :] + kept[chunk - 3 :] if chunk >= 2 else []
            source, *_ = lax.optimization_barrier((gated, *behind))
            far = project(source, out_weight, cols(2, zero, chunk), width)
            summed.append((shift(far[0], "x", 1), shift(far[1], "x", -1)))
        if 1 <= chunk <= CHUNKS:
            at = chunk - 1
            from_left, from_right = summed[at]
            source, *_ = lax.optimization_barrier((gated, *swapped[at - 3 :])) if at >= 3 else (gated,)
            right = project(source, out_weight, cols(1, zero, at), width, (0,), (from_left,), True)
            left = project(source, out_weight, cols(-1, zero, at), width, (1,), (from_right,), True)
            summed[at] = (right, left)
        if chunk >= 2:
            at = chunk - 2
            right, left = summed[at]
            terms = (shift(right, "x", 1), shift(left, "x", -1))
            keep, send = project_own(gated, out_weight, cols(0, z_index, at), width, z_index, terms)
            kept.append(send)
            swapped.append(shift(send, "zh", 1))
            outs.append(keep + swapped[at])
    return jnp.concatenate(outs, axis=1).astype(jnp.bfloat16)


def solution(mesh):
    sizes = [size for _, size in SEQ_PARTS + CHAN_PARTS]
    parts = Mesh(mesh.devices.reshape(sizes), SEQ + CHAN)
    in_specs = (
        P(SEQ, CHAN),
        P(SEQ, CHAN),
        P(SEQ, CHAN),
        P(CHAN, None),
        P(CHAN, None),
        P(CHAN),
        P(CHAN, None),
    )
    return jax.shard_map(
        per_device, mesh=parts, in_specs=in_specs, out_specs=P(SEQ, CHAN), check_vma=False
    )
```

```python
import functools

import jax
import jax.numpy as jnp
from jax import lax
from jax.experimental import pallas as pl
from jax.experimental.pallas import tpu as pltpu
from jax.sharding import Mesh
from jax.sharding import PartitionSpec as P

F32 = jnp.float32
LANES = 128
SUBS = 8
ALL_VMEM = 56 * 1024 * 1024
MOST_VMEM = 52 * 1024 * 1024
GATE_VMEM = 56 * 1024 * 1024
WIDTHS = (256, 256)
SEQ_PARTS = (("y", 4), ("zl", 8), ("core", 2))
CHAN_PARTS = (("x", 4), ("zh", 2))
SEQ = tuple(name for name, _ in SEQ_PARTS)
CHAN = tuple(name for name, _ in CHAN_PARTS)


def tree_sum(terms):
    while len(terms) > 1:
        terms = [a + b for a, b in zip(terms[::2], terms[1::2])]
    return terms[0]


def whole_call(kernel, out_shape, scratch_shapes, vmem, args, in_specs=None):
    return pl.pallas_call(
        kernel,
        in_specs=in_specs or [pl.BlockSpec(memory_space=pltpu.VMEM)] * len(args),
        out_specs=jax.tree.map(lambda _: pl.BlockSpec(memory_space=pltpu.VMEM), out_shape),
        out_shape=out_shape,
        scratch_shapes=scratch_shapes,
        compiler_params=pltpu.CompilerParams(vmem_limit_bytes=vmem),
        cost_estimate=pl.CostEstimate(flops=1 << 24, bytes_accessed=1 << 21, transcendentals=0),
    )(*args)


def mix_into(x_ref, k_ref, v_ref):
    tokens, chans = k_ref.shape
    for tile in range(chans // LANES):
        lanes = pl.ds(tile * LANES, LANES)
        x_ref[pl.ds(tile * tokens, tokens), :] = k_ref[:, lanes].astype(F32) * v_ref[:, lanes].astype(F32)


def spread_row(ref, row, lanes):
    return jnp.broadcast_to(ref[row : row + 1, lanes], (SUBS, LANES))


def state_kernel(length, *refs):
    hbm, refs = refs[:4], refs[4:]
    rate_ref, coef_ref, ends_ref, state_ref, fade_ref, x_ref, *arrived, sems = refs
    copies = [pltpu.make_async_copy(src, dst, sems.at[i]) for i, (src, dst) in enumerate(zip(hbm, arrived))]
    for copy in copies:
        copy.start()
    for copy in copies:
        copy.wait()
    k_ref, v_ref, decay_ref, res_ref = arrived
    tokens, chans = k_ref.shape
    modes = rate_ref.shape[0]
    run = tokens // SUBS
    mix_into(x_ref, k_ref, v_ref)
    rate = decay_ref[...] / length
    rate_ref[...] = rate
    coef_ref[...] = res_ref[...] * jnp.sqrt(2.0 * rate)
    later = (SUBS - 1 - lax.broadcasted_iota(jnp.int32, (SUBS, LANES), 0)).astype(F32) * run
    for tile in range(chans // LANES):
        lanes = pl.ds(tile * LANES, LANES)
        rates = [spread_row(rate_ref, m, lanes) for m in range(modes)]
        steps = [jnp.exp(-r) for r in rates]

        def body(j, held, base=tile * tokens):
            x = x_ref[pl.ds(base + j, SUBS, stride=run), :]
            return tuple(a * h + x for a, h in zip(steps, held))

        held = tuple(jnp.zeros((SUBS, LANES), F32) for _ in range(modes))
        held = lax.fori_loop(0, run, body, held, unroll=8)
        for m in range(modes):
            ends_ref[m, :, lanes] = held[m]
            row = m * (chans // LANES) + tile
            state_ref[row : row + 1, :] = jnp.sum(held[m] * jnp.exp(-rates[m] * later), axis=0, keepdims=True)
            fade_ref[row : row + 1, :] = jnp.exp(-rates[m][:1] * tokens)


def local_kernel(x_ref, rate_ref, coef_ref, ends_ref, skip_ref, out_ref, y_ref):
    chans = rate_ref.shape[1]
    tokens = x_ref.shape[0] * LANES // chans
    modes = rate_ref.shape[0]
    run = tokens // SUBS
    place = lax.broadcasted_iota(jnp.int32, (SUBS, LANES), 0)

    def down(value, by):
        return jnp.where(place >= by, pltpu.roll(value, by, 0), 0.0)

    for tile in range(chans // LANES):
        lanes = pl.ds(tile * LANES, LANES)
        steps, held = [], []
        for m in range(modes):
            rate = spread_row(rate_ref, m, lanes)
            steps.append(jnp.exp(-rate))
            total = ends_ref[m, :, lanes]
            for by in (1, 2, 4):
                total = total + jnp.exp(-rate * (by * run)) * down(total, by)
            held.append(down(total, 1))
        coefs = [spread_row(coef_ref, m, lanes) for m in range(modes)]

        def body(j, held, base=tile * tokens):
            x = x_ref[pl.ds(base + j, SUBS, stride=run), :]
            held = tuple(a * h + x for a, h in zip(steps, held))
            y_ref[pl.ds(base + j, SUBS, stride=run), :] = tree_sum([c * h for c, h in zip(coefs, held)])
            return held

        lax.fori_loop(0, run, body, tuple(held), unroll=4)
        rows = pl.ds(tile * tokens, tokens)
        out_ref[rows, :] = y_ref[rows, :] + skip_ref[:, lanes] * x_ref[rows, :]


def gate_kernel(cols_ref, q_ref, local_ref, rate_ref, coef_ref, enter_ref, weight_ref, *refs):
    out_ref, far_ref, near_ref, y_ref, block_ref, sems = refs
    fetches = start_fetches(cols_ref, weight_ref, block_ref, sems)
    tokens, chans = q_ref.shape
    modes = rate_ref.shape[0]
    run = tokens // SUBS
    place = (lax.broadcasted_iota(jnp.int32, (SUBS, LANES), 0) * run + 1).astype(F32)
    for tile in range(chans // LANES):
        lanes = pl.ds(tile * LANES, LANES)
        steps, held = [], []
        for m in range(modes):
            rate = spread_row(rate_ref, m, lanes)
            steps.append(jnp.exp(-rate))
            weight = spread_row(coef_ref, m, lanes) * spread_row(enter_ref, m * (chans // LANES) + tile, slice(None))
            held.append(weight * jnp.exp(-rate * place))

        def body(j, held, base=tile * tokens):
            y_ref[pl.ds(base + j, SUBS, stride=run), :] = tree_sum(list(held))
            return tuple(a * h for a, h in zip(steps, held))

        lax.fori_loop(0, run, body, tuple(held), unroll=4)
        rows = pl.ds(tile * tokens, tokens)
        value = q_ref[:, lanes].astype(F32) * (local_ref[rows, :] + y_ref[rows, :])
        out_ref[:, lanes] = value.astype(out_ref.dtype)
    multiply(fetches, out_ref, block_ref, (far_ref, near_ref))


def start_fetches(cols_ref, weight_ref, block_ref, sems):
    fetches = []
    for i in range(block_ref.shape[0]):
        lanes = pl.ds(pl.multiple_of(cols_ref[i] * LANES, LANES), block_ref.shape[2])
        fetches.append(pltpu.make_async_copy(weight_ref.at[:, lanes], block_ref.at[i], sems.at[i]))
        fetches[-1].start()
    return fetches


def multiply(fetches, gated_ref, block_ref, outs, adds=()):
    for i, fetch in enumerate(fetches):
        fetch.wait()
        block = jnp.dot(gated_ref[...], block_ref[i], preferred_element_type=F32)
        for add in adds:
            block = block + add[i]
        outs[i // 2][i % 2] = block


def project_kernel(count, cols_ref, gated_ref, weight_ref, *refs):
    adds, outs, (block_ref, sems) = refs[: -2 - count], refs[-2 - count : -2], refs[-2:]
    multiply(start_fetches(cols_ref, weight_ref, block_ref, sems), gated_ref, block_ref, outs, adds)


def own_kernel(cols_ref, gated_ref, weight_ref, left_ref, right_ref, keep_ref, send_ref, block_ref, sems):
    fetches = start_fetches(cols_ref, weight_ref, block_ref, sems)
    mine = cols_ref[2]
    for half, at, out in ((1, 1 - mine, send_ref), (0, mine, keep_ref)):
        fetches[half].wait()
        block = jnp.dot(gated_ref[...], block_ref[half], preferred_element_type=F32)
        out[...] = block + left_ref[at] + right_ref[at]


def fetched(weight, blocks, width):
    return [pltpu.VMEM((blocks, weight.shape[0], width), weight.dtype), pltpu.SemaphoreType.DMA((blocks,))]


def project_call(kernel, shapes, blocks, width, cols, gated, weight, terms):
    vmem = pl.BlockSpec(memory_space=pltpu.VMEM)
    specs = [pl.BlockSpec(memory_space=pltpu.SMEM), vmem, pl.BlockSpec(memory_space=pl.ANY)] + [vmem] * len(terms)
    return whole_call(kernel, shapes, fetched(weight, blocks, width), MOST_VMEM, (cols, gated, weight, *terms), specs)


def shift(value, axis, by):
    size = lax.axis_size(axis)
    return lax.ppermute(value, axis, [(i, (i + by) % size) for i in range(size)])


def scan_kernel(state_ref, fade_ref, enter_ref):
    count, total = fade_ref.shape[0], jnp.zeros(fade_ref.shape, F32)
    for first in range(0, state_ref.shape[0], count):
        enter_ref[first : first + count, :] = total
        total = total * fade_ref[...] + state_ref[first : first + count, :]


def entering_states(state, fade):
    count, index = state.shape[0], jnp.int32(0)
    for axis in SEQ:
        count = count // lax.axis_size(axis)
        index = index * lax.axis_size(axis) + lax.axis_index(axis)
    fade = lax.dynamic_slice_in_dim(fade, index * count, count, 0)
    state = lax.all_to_all(state, SEQ, 0, 0, tiled=True)
    enter = whole_call(scan_kernel, jax.ShapeDtypeStruct(state.shape, F32), [], MOST_VMEM, (state, fade))
    return lax.all_to_all(enter, SEQ, 0, 0, tiled=True)


def per_device(queries, key_proj, value_proj, decay_rate, residues, skip_gain, out_weight):
    tokens, chans = queries.shape
    modes = decay_rate.shape[1]
    seq_size = 1
    for axis in SEQ:
        seq_size *= lax.axis_size(axis)
    small = jax.ShapeDtypeStruct((modes, chans), F32)
    stacked = jax.ShapeDtypeStruct((tokens * chans // LANES, LANES), F32)
    args = (key_proj, value_proj, decay_rate.T, residues.T)
    ends = jax.ShapeDtypeStruct((modes, SUBS, chans), F32)
    rows = jax.ShapeDtypeStruct((modes * chans // LANES, LANES), F32)
    rate, coef, ends, state, fade, mixed = whole_call(
        functools.partial(state_kernel, float(tokens * seq_size)),
        (small, small, ends, rows, rows, stacked),
        [pltpu.VMEM(a.shape, a.dtype) for a in args] + [pltpu.SemaphoreType.DMA((len(args),))],
        ALL_VMEM,
        args,
        [pl.BlockSpec(memory_space=pl.ANY)] * len(args),
    )
    scratch = [pltpu.VMEM(stacked.shape, F32)]
    local = whole_call(local_kernel, stacked, scratch, ALL_VMEM, (mixed, rate, coef, ends, skip_gain[None, :]))
    enter = entering_states(state, fade)
    x_size, x_index = lax.axis_size("x"), lax.axis_index("x")
    z_size, z_index = lax.axis_size("zh"), lax.axis_index("zh").astype(jnp.int32)
    features = out_weight.shape[1] // (x_size * z_size)

    def cols(x_bys, chunk, first=jnp.int32(0)):
        lanes = []
        for x_by in x_bys:
            start = ((x_index + x_by) % x_size) * z_size
            lanes += [(start + z) * features + sum(WIDTHS[:chunk]) for z in (first, 1 - first)]
        return (jnp.stack(lanes) // LANES).astype(jnp.int32)

    def pair(chunk):
        return jax.ShapeDtypeStruct((2, tokens, WIDTHS[chunk]), F32)

    vmem, anywhere = pl.BlockSpec(memory_space=pltpu.VMEM), pl.BlockSpec(memory_space=pl.ANY)
    gated, far, near = whole_call(
        gate_kernel,
        (jax.ShapeDtypeStruct((tokens, chans), queries.dtype), pair(0), pair(0)),
        scratch + fetched(out_weight, 4, WIDTHS[0]),
        GATE_VMEM,
        (cols((2, -1), 0), queries, local, rate, coef, enter, out_weight),
        [pl.BlockSpec(memory_space=pltpu.SMEM)] + [vmem] * 5 + [anywhere],
    )
    ways = [1 if chunk % 2 == 0 else -1 for chunk in range(len(WIDTHS))]
    firsts = []
    for chunk, way in enumerate(ways):
        if chunk:
            kernel = functools.partial(project_kernel, 2)
            at = cols((2, -way), chunk)
            far, near = project_call(
                kernel, (pair(chunk), pair(chunk)), 4, WIDTHS[chunk], at, gated, out_weight, ()
            )
        firsts.append((shift(far, "x", way), near))
    seconds = []
    for chunk, way in enumerate(ways):
        passed, near = firsts[chunk]
        kernel = functools.partial(project_kernel, 1)
        (both,) = project_call(
            kernel, (pair(chunk),), 2, WIDTHS[chunk], cols((way,), chunk), gated, out_weight, (passed,)
        )
        seconds.append((shift(both, "x", way), shift(near, "x", -way)))
    outs = []
    for chunk, terms in enumerate(seconds):
        at = jnp.concatenate([cols((0,), chunk, z_index), z_index[None]])
        block = jax.ShapeDtypeStruct((tokens, WIDTHS[chunk]), F32)
        keep, send = project_call(own_kernel, (block, block), 2, WIDTHS[chunk], at, gated, out_weight, terms)
        outs.append(keep + shift(send, "zh", 1))
    return jnp.concatenate(outs, axis=1).astype(jnp.bfloat16)


def solution(mesh):
    sizes = [size for _, size in SEQ_PARTS + CHAN_PARTS]
    parts = Mesh(mesh.devices.reshape(sizes), SEQ + CHAN)
    in_specs = (
        P(SEQ, CHAN),
        P(SEQ, CHAN),
        P(SEQ, CHAN),
        P(CHAN, None),
        P(CHAN, None),
        P(CHAN),
        P(CHAN, None),
    )
    return jax.shard_map(
        per_device, mesh=parts, in_specs=in_specs, out_specs=P(SEQ, CHAN), check_vma=False
    )
```

```python
import functools

import jax
import jax.numpy as jnp
from jax import lax
from jax.experimental import pallas as pl
from jax.experimental.pallas import tpu as pltpu
from jax.sharding import Mesh
from jax.sharding import PartitionSpec as P

F32 = jnp.float32
LANES = 128
SUBS = 8
ALL_VMEM = 56 * 1024 * 1024
MOST_VMEM = 52 * 1024 * 1024
GATE_VMEM = 56 * 1024 * 1024
WIDTHS = (256, 256)
SEQ_PARTS = (("y", 4), ("zl", 8), ("core", 2))
CHAN_PARTS = (("x", 4), ("zh", 2))
SEQ = tuple(name for name, _ in SEQ_PARTS)
CHAN = tuple(name for name, _ in CHAN_PARTS)


def tree_sum(terms):
    while len(terms) > 1:
        terms = [a + b for a, b in zip(terms[::2], terms[1::2])]
    return terms[0]


def whole_call(kernel, out_shape, scratch_shapes, vmem, args, in_specs=None):
    return pl.pallas_call(
        kernel,
        in_specs=in_specs or [pl.BlockSpec(memory_space=pltpu.VMEM)] * len(args),
        out_specs=jax.tree.map(lambda _: pl.BlockSpec(memory_space=pltpu.VMEM), out_shape),
        out_shape=out_shape,
        scratch_shapes=scratch_shapes,
        compiler_params=pltpu.CompilerParams(vmem_limit_bytes=vmem),
        cost_estimate=pl.CostEstimate(flops=1 << 24, bytes_accessed=1 << 21, transcendentals=0),
    )(*args)


def mix_into(x_ref, k_ref, v_ref):
    tokens, chans = k_ref.shape
    for tile in range(chans // LANES):
        lanes = pl.ds(tile * LANES, LANES)
        x_ref[pl.ds(tile * tokens, tokens), :] = k_ref[:, lanes].astype(F32) * v_ref[:, lanes].astype(F32)


def spread_row(ref, row, lanes):
    return jnp.broadcast_to(ref[row : row + 1, lanes], (SUBS, LANES))


def state_kernel(length, *refs):
    hbm, refs = refs[:4], refs[4:]
    rate_ref, coef_ref, ends_ref, state_ref, x_ref, *arrived, sems = refs
    copies = [pltpu.make_async_copy(src, dst, sems.at[i]) for i, (src, dst) in enumerate(zip(hbm, arrived))]
    for copy in copies:
        copy.start()
    for copy in copies:
        copy.wait()
    k_ref, v_ref, decay_ref, res_ref = arrived
    tokens, chans = k_ref.shape
    modes = rate_ref.shape[0]
    run = tokens // SUBS
    mix_into(x_ref, k_ref, v_ref)
    rate = decay_ref[...] / length
    rate_ref[...] = rate
    coef_ref[...] = res_ref[...] * jnp.sqrt(2.0 * rate)
    later = (SUBS - 1 - lax.broadcasted_iota(jnp.int32, (SUBS, LANES), 0)).astype(F32) * run
    for tile in range(chans // LANES):
        lanes = pl.ds(tile * LANES, LANES)
        rates = [spread_row(rate_ref, m, lanes) for m in range(modes)]
        steps = [jnp.exp(-r) for r in rates]

        def body(j, held, base=tile * tokens):
            x = x_ref[pl.ds(base + j, SUBS, stride=run), :]
            return tuple(a * h + x for a, h in zip(steps, held))

        held = tuple(jnp.zeros((SUBS, LANES), F32) for _ in range(modes))
        held = lax.fori_loop(0, run, body, held, unroll=8)
        for m in range(modes):
            ends_ref[m, :, lanes] = held[m]
            state_ref[m : m + 1, lanes] = jnp.sum(
                held[m] * jnp.exp(-rates[m] * later), axis=0, keepdims=True
            )


def local_kernel(x_ref, rate_ref, coef_ref, ends_ref, skip_ref, out_ref, y_ref):
    chans = rate_ref.shape[1]
    tokens = x_ref.shape[0] * LANES // chans
    modes = rate_ref.shape[0]
    run = tokens // SUBS
    place = lax.broadcasted_iota(jnp.int32, (SUBS, LANES), 0)

    def down(value, by):
        return jnp.where(place >= by, pltpu.roll(value, by, 0), 0.0)

    for tile in range(chans // LANES):
        lanes = pl.ds(tile * LANES, LANES)
        steps, held = [], []
        for m in range(modes):
            rate = spread_row(rate_ref, m, lanes)
            steps.append(jnp.exp(-rate))
            total = ends_ref[m, :, lanes]
            for by in (1, 2, 4):
                total = total + jnp.exp(-rate * (by * run)) * down(total, by)
            held.append(down(total, 1))
        coefs = [spread_row(coef_ref, m, lanes) for m in range(modes)]

        def body(j, held, base=tile * tokens):
            x = x_ref[pl.ds(base + j, SUBS, stride=run), :]
            held = tuple(a * h + x for a, h in zip(steps, held))
            y_ref[pl.ds(base + j, SUBS, stride=run), :] = tree_sum([c * h for c, h in zip(coefs, held)])
            return held

        lax.fori_loop(0, run, body, tuple(held), unroll=4)
        rows = pl.ds(tile * tokens, tokens)
        out_ref[rows, :] = y_ref[rows, :] + skip_ref[:, lanes] * x_ref[rows, :]


def gate_kernel(cols_ref, q_ref, local_ref, rate_ref, coef_ref, enter_ref, weight_ref, *refs):
    out_ref, far_ref, near_ref, y_ref, block_ref, sems = refs
    fetches = start_fetches(cols_ref, weight_ref, block_ref, sems)
    tokens, chans = q_ref.shape
    modes = rate_ref.shape[0]
    run = tokens // SUBS
    place = (lax.broadcasted_iota(jnp.int32, (SUBS, LANES), 0) * run + 1).astype(F32)
    for tile in range(chans // LANES):
        lanes = pl.ds(tile * LANES, LANES)
        steps, held = [], []
        for m in range(modes):
            rate = spread_row(rate_ref, m, lanes)
            steps.append(jnp.exp(-rate))
            weight = spread_row(coef_ref, m, lanes) * spread_row(enter_ref, m, lanes)
            held.append(weight * jnp.exp(-rate * place))

        def body(j, held, base=tile * tokens):
            y_ref[pl.ds(base + j, SUBS, stride=run), :] = tree_sum(list(held))
            return tuple(a * h for a, h in zip(steps, held))

        lax.fori_loop(0, run, body, tuple(held), unroll=4)
        rows = pl.ds(tile * tokens, tokens)
        value = q_ref[:, lanes].astype(F32) * (local_ref[rows, :] + y_ref[rows, :])
        out_ref[:, lanes] = value.astype(out_ref.dtype)
    multiply(fetches, out_ref, block_ref, (far_ref, near_ref))


def start_fetches(cols_ref, weight_ref, block_ref, sems):
    fetches = []
    for i in range(block_ref.shape[0]):
        lanes = pl.ds(pl.multiple_of(cols_ref[i] * LANES, LANES), block_ref.shape[2])
        fetches.append(pltpu.make_async_copy(weight_ref.at[:, lanes], block_ref.at[i], sems.at[i]))
        fetches[-1].start()
    return fetches


def multiply(fetches, gated_ref, block_ref, outs, adds=()):
    for i, fetch in enumerate(fetches):
        fetch.wait()
        block = jnp.dot(gated_ref[...], block_ref[i], preferred_element_type=F32)
        for add in adds:
            block = block + add[i]
        outs[i // 2][i % 2] = block


def project_kernel(count, cols_ref, gated_ref, weight_ref, *refs):
    adds, outs, (block_ref, sems) = refs[: -2 - count], refs[-2 - count : -2], refs[-2:]
    multiply(start_fetches(cols_ref, weight_ref, block_ref, sems), gated_ref, block_ref, outs, adds)


def own_kernel(cols_ref, gated_ref, weight_ref, left_ref, right_ref, keep_ref, send_ref, block_ref, sems):
    fetches = start_fetches(cols_ref, weight_ref, block_ref, sems)
    mine = cols_ref[2]
    for half, at, out in ((1, 1 - mine, send_ref), (0, mine, keep_ref)):
        fetches[half].wait()
        block = jnp.dot(gated_ref[...], block_ref[half], preferred_element_type=F32)
        out[...] = block + left_ref[at] + right_ref[at]


def fetched(weight, blocks, width):
    return [pltpu.VMEM((blocks, weight.shape[0], width), weight.dtype), pltpu.SemaphoreType.DMA((blocks,))]


def project_call(kernel, shapes, blocks, width, cols, gated, weight, terms):
    vmem = pl.BlockSpec(memory_space=pltpu.VMEM)
    specs = [pl.BlockSpec(memory_space=pltpu.SMEM), vmem, pl.BlockSpec(memory_space=pl.ANY)] + [vmem] * len(terms)
    return whole_call(kernel, shapes, fetched(weight, blocks, width), MOST_VMEM, (cols, gated, weight, *terms), specs)


def shift(value, axis, by):
    size = lax.axis_size(axis)
    return lax.ppermute(value, axis, [(i, (i + by) % size) for i in range(size)])


def entering_states(state, rate, tokens):
    enter, total = jnp.zeros_like(state), state
    offset, span = jnp.int32(0), 1
    for axis in reversed(SEQ[1:]):
        size, index = lax.axis_size(axis), lax.axis_index(axis)
        by = 1
        while by < size:
            other = lax.ppermute(total, axis, [(i, i ^ by) for i in range(size)])
            upper = (index & by) != 0
            enter = enter + jnp.where(upper, jnp.exp(-rate * (offset * tokens).astype(F32)) * other, 0.0)
            fade = jnp.exp(-rate * float(span * tokens))
            total = jnp.where(upper, total + fade * other, other + fade * total)
            offset = offset + jnp.where(upper, span, 0)
            span, by = span * 2, by * 2
    size, index = lax.axis_size(SEQ[0]), lax.axis_index(SEQ[0])
    copies = jnp.broadcast_to(total, (size, *total.shape))
    totals = lax.all_to_all(copies, SEQ[0], 0, 0, tiled=True)
    fade, before = jnp.exp(-rate * float(span * tokens)), jnp.zeros_like(state)
    for block in range(size - 1):
        before = jnp.where(block < index, before * fade + totals[block], before)
    return enter + jnp.exp(-rate * (offset * tokens).astype(F32)) * before


def per_device(queries, key_proj, value_proj, decay_rate, residues, skip_gain, out_weight):
    tokens, chans = queries.shape
    modes = decay_rate.shape[1]
    seq_size = 1
    for axis in SEQ:
        seq_size *= lax.axis_size(axis)
    small = jax.ShapeDtypeStruct((modes, chans), F32)
    stacked = jax.ShapeDtypeStruct((tokens * chans // LANES, LANES), F32)
    args = (key_proj, value_proj, decay_rate.T, residues.T)
    ends = jax.ShapeDtypeStruct((modes, SUBS, chans), F32)
    rate, coef, ends, state, mixed = whole_call(
        functools.partial(state_kernel, float(tokens * seq_size)),
        (small, small, ends, small, stacked),
        [pltpu.VMEM(a.shape, a.dtype) for a in args] + [pltpu.SemaphoreType.DMA((len(args),))],
        ALL_VMEM,
        args,
        [pl.BlockSpec(memory_space=pl.ANY)] * len(args),
    )
    scratch = [pltpu.VMEM(stacked.shape, F32)]
    local = whole_call(local_kernel, stacked, scratch, ALL_VMEM, (mixed, rate, coef, ends, skip_gain[None, :]))
    enter = entering_states(state, rate, tokens)
    x_size, x_index = lax.axis_size("x"), lax.axis_index("x")
    z_size, z_index = lax.axis_size("zh"), lax.axis_index("zh").astype(jnp.int32)
    features = out_weight.shape[1] // (x_size * z_size)

    def cols(x_bys, chunk, first=jnp.int32(0)):
        lanes = []
        for x_by in x_bys:
            start = ((x_index + x_by) % x_size) * z_size
            lanes += [(start + z) * features + sum(WIDTHS[:chunk]) for z in (first, 1 - first)]
        return (jnp.stack(lanes) // LANES).astype(jnp.int32)

    def pair(chunk):
        return jax.ShapeDtypeStruct((2, tokens, WIDTHS[chunk]), F32)

    vmem, anywhere = pl.BlockSpec(memory_space=pltpu.VMEM), pl.BlockSpec(memory_space=pl.ANY)
    gated, far, near = whole_call(
        gate_kernel,
        (jax.ShapeDtypeStruct((tokens, chans), queries.dtype), pair(0), pair(0)),
        scratch + fetched(out_weight, 4, WIDTHS[0]),
        GATE_VMEM,
        (cols((2, -1), 0), queries, local, rate, coef, enter, out_weight),
        [pl.BlockSpec(memory_space=pltpu.SMEM)] + [vmem] * 5 + [anywhere],
    )
    ways = [1 if chunk % 2 == 0 else -1 for chunk in range(len(WIDTHS))]
    firsts = []
    for chunk, way in enumerate(ways):
        if chunk:
            kernel = functools.partial(project_kernel, 2)
            at = cols((2, -way), chunk)
            far, near = project_call(
                kernel, (pair(chunk), pair(chunk)), 4, WIDTHS[chunk], at, gated, out_weight, ()
            )
        firsts.append((shift(far, "x", way), near))
    seconds = []
    for chunk, way in enumerate(ways):
        passed, near = firsts[chunk]
        kernel = functools.partial(project_kernel, 1)
        (both,) = project_call(
            kernel, (pair(chunk),), 2, WIDTHS[chunk], cols((way,), chunk), gated, out_weight, (passed,)
        )
        seconds.append((shift(both, "x", way), shift(near, "x", -way)))
    outs = []
    for chunk, terms in enumerate(seconds):
        at = jnp.concatenate([cols((0,), chunk, z_index), z_index[None]])
        block = jax.ShapeDtypeStruct((tokens, WIDTHS[chunk]), F32)
        keep, send = project_call(own_kernel, (block, block), 2, WIDTHS[chunk], at, gated, out_weight, terms)
        outs.append(keep + shift(send, "zh", 1))
    return jnp.concatenate(outs, axis=1).astype(jnp.bfloat16)


def solution(mesh):
    sizes = [size for _, size in SEQ_PARTS + CHAN_PARTS]
    parts = Mesh(mesh.devices.reshape(sizes), SEQ + CHAN)
    in_specs = (
        P(SEQ, CHAN),
        P(SEQ, CHAN),
        P(SEQ, CHAN),
        P(CHAN, None),
        P(CHAN, None),
        P(CHAN),
        P(CHAN, None),
    )
    return jax.shard_map(
        per_device, mesh=parts, in_specs=in_specs, out_specs=P(SEQ, CHAN), check_vma=False
    )
```

```python
import functools

import jax
import jax.numpy as jnp
from jax import lax
from jax.experimental import pallas as pl
from jax.experimental.pallas import tpu as pltpu
from jax.sharding import Mesh
from jax.sharding import PartitionSpec as P

F32 = jnp.float32
LANES = 128
SUBS = 8
ALL_VMEM = 56 * 1024 * 1024
MOST_VMEM = 52 * 1024 * 1024
GATE_VMEM = 56 * 1024 * 1024
WIDTHS = (256, 256)
SEQ_PARTS = (("y", 4), ("zl", 8), ("core", 2))
CHAN_PARTS = (("x", 4), ("zh", 2))
SEQ = tuple(name for name, _ in SEQ_PARTS)
CHAN = tuple(name for name, _ in CHAN_PARTS)


def tree_sum(terms):
    while len(terms) > 1:
        terms = [a + b for a, b in zip(terms[::2], terms[1::2])]
    return terms[0]


def whole_call(kernel, out_shape, scratch_shapes, vmem, args, in_specs=None):
    return pl.pallas_call(
        kernel,
        in_specs=in_specs or [pl.BlockSpec(memory_space=pltpu.VMEM)] * len(args),
        out_specs=jax.tree.map(lambda _: pl.BlockSpec(memory_space=pltpu.VMEM), out_shape),
        out_shape=out_shape,
        scratch_shapes=scratch_shapes,
        compiler_params=pltpu.CompilerParams(vmem_limit_bytes=vmem),
        cost_estimate=pl.CostEstimate(flops=1 << 24, bytes_accessed=1 << 21, transcendentals=0),
    )(*args)


def mix_into(x_ref, k_ref, v_ref):
    tokens, chans = k_ref.shape
    for tile in range(chans // LANES):
        lanes = pl.ds(tile * LANES, LANES)
        x_ref[pl.ds(tile * tokens, tokens), :] = k_ref[:, lanes].astype(F32) * v_ref[:, lanes].astype(F32)


def spread_row(ref, row, lanes):
    return jnp.broadcast_to(ref[row : row + 1, lanes], (SUBS, LANES))


def state_kernel(length, *refs):
    hbm, refs = refs[:4], refs[4:]
    rate_ref, coef_ref, ends_ref, state_ref, x_ref, *arrived, sems = refs
    copies = [pltpu.make_async_copy(src, dst, sems.at[i]) for i, (src, dst) in enumerate(zip(hbm, arrived))]
    for copy in copies:
        copy.start()
    for copy in copies:
        copy.wait()
    k_ref, v_ref, decay_ref, res_ref = arrived
    tokens, chans = k_ref.shape
    modes = rate_ref.shape[0]
    run = tokens // SUBS
    mix_into(x_ref, k_ref, v_ref)
    rate = decay_ref[...] / length
    rate_ref[...] = rate
    coef_ref[...] = res_ref[...] * jnp.sqrt(2.0 * rate)
    later = (SUBS - 1 - lax.broadcasted_iota(jnp.int32, (SUBS, LANES), 0)).astype(F32) * run
    for tile in range(chans // LANES):
        lanes = pl.ds(tile * LANES, LANES)
        rates = [spread_row(rate_ref, m, lanes) for m in range(modes)]
        steps = [jnp.exp(-r) for r in rates]

        def body(j, held, base=tile * tokens):
            x = x_ref[pl.ds(base + j, SUBS, stride=run), :]
            return tuple(a * h + x for a, h in zip(steps, held))

        held = tuple(jnp.zeros((SUBS, LANES), F32) for _ in range(modes))
        held = lax.fori_loop(0, run, body, held, unroll=8)
        for m in range(modes):
            ends_ref[m, :, lanes] = held[m]
            state_ref[m : m + 1, lanes] = jnp.sum(
                held[m] * jnp.exp(-rates[m] * later), axis=0, keepdims=True
            )


def local_kernel(x_ref, rate_ref, coef_ref, ends_ref, skip_ref, out_ref, y_ref):
    chans = rate_ref.shape[1]
    tokens = x_ref.shape[0] * LANES // chans
    modes = rate_ref.shape[0]
    run = tokens // SUBS
    place = lax.broadcasted_iota(jnp.int32, (SUBS, LANES), 0)

    def down(value, by):
        return jnp.where(place >= by, pltpu.roll(value, by, 0), 0.0)

    for tile in range(chans // LANES):
        lanes = pl.ds(tile * LANES, LANES)
        steps, held = [], []
        for m in range(modes):
            rate = spread_row(rate_ref, m, lanes)
            steps.append(jnp.exp(-rate))
            total = ends_ref[m, :, lanes]
            for by in (1, 2, 4):
                total = total + jnp.exp(-rate * (by * run)) * down(total, by)
            held.append(down(total, 1))
        coefs = [spread_row(coef_ref, m, lanes) for m in range(modes)]

        def body(j, held, base=tile * tokens):
            x = x_ref[pl.ds(base + j, SUBS, stride=run), :]
            held = tuple(a * h + x for a, h in zip(steps, held))
            y_ref[pl.ds(base + j, SUBS, stride=run), :] = tree_sum([c * h for c, h in zip(coefs, held)])
            return held

        lax.fori_loop(0, run, body, tuple(held), unroll=4)
        rows = pl.ds(tile * tokens, tokens)
        out_ref[rows, :] = y_ref[rows, :] + skip_ref[:, lanes] * x_ref[rows, :]


def gate_kernel(cols_ref, q_ref, local_ref, rate_ref, coef_ref, enter_ref, weight_ref, *refs):
    out_ref, far_ref, near_ref, y_ref, block_ref, sems = refs
    fetches = start_fetches(cols_ref, weight_ref, block_ref, sems)
    tokens, chans = q_ref.shape
    modes = rate_ref.shape[0]
    run = tokens // SUBS
    place = (lax.broadcasted_iota(jnp.int32, (SUBS, LANES), 0) * run + 1).astype(F32)
    for tile in range(chans // LANES):
        lanes = pl.ds(tile * LANES, LANES)
        steps, held = [], []
        for m in range(modes):
            rate = spread_row(rate_ref, m, lanes)
            steps.append(jnp.exp(-rate))
            weight = spread_row(coef_ref, m, lanes) * spread_row(enter_ref, m, lanes)
            held.append(weight * jnp.exp(-rate * place))

        def body(j, held, base=tile * tokens):
            y_ref[pl.ds(base + j, SUBS, stride=run), :] = tree_sum(list(held))
            return tuple(a * h for a, h in zip(steps, held))

        lax.fori_loop(0, run, body, tuple(held), unroll=4)
        rows = pl.ds(tile * tokens, tokens)
        value = q_ref[:, lanes].astype(F32) * (local_ref[rows, :] + y_ref[rows, :])
        out_ref[:, lanes] = value.astype(out_ref.dtype)
    multiply(fetches, out_ref, block_ref, (far_ref, near_ref))


def start_fetches(cols_ref, weight_ref, block_ref, sems):
    fetches = []
    for i in range(block_ref.shape[0]):
        lanes = pl.ds(pl.multiple_of(cols_ref[i] * LANES, LANES), block_ref.shape[2])
        fetches.append(pltpu.make_async_copy(weight_ref.at[:, lanes], block_ref.at[i], sems.at[i]))
        fetches[-1].start()
    return fetches


def multiply(fetches, gated_ref, block_ref, outs, adds=()):
    for i, fetch in enumerate(fetches):
        fetch.wait()
        block = jnp.dot(gated_ref[...], block_ref[i], preferred_element_type=F32)
        for add in adds:
            block = block + add[i]
        outs[i // 2][i % 2] = block


def project_kernel(count, cols_ref, gated_ref, weight_ref, *refs):
    adds, outs, (block_ref, sems) = refs[: -2 - count], refs[-2 - count : -2], refs[-2:]
    multiply(start_fetches(cols_ref, weight_ref, block_ref, sems), gated_ref, block_ref, outs, adds)


def own_kernel(cols_ref, gated_ref, weight_ref, left_ref, right_ref, keep_ref, send_ref, block_ref, sems):
    fetches = start_fetches(cols_ref, weight_ref, block_ref, sems)
    mine = cols_ref[2]
    for half, at, out in ((1, 1 - mine, send_ref), (0, mine, keep_ref)):
        fetches[half].wait()
        block = jnp.dot(gated_ref[...], block_ref[half], preferred_element_type=F32)
        out[...] = block + left_ref[at] + right_ref[at]


def fetched(weight, blocks, width):
    return [pltpu.VMEM((blocks, weight.shape[0], width), weight.dtype), pltpu.SemaphoreType.DMA((blocks,))]


def project_call(kernel, shapes, blocks, width, cols, gated, weight, terms):
    vmem = pl.BlockSpec(memory_space=pltpu.VMEM)
    specs = [pl.BlockSpec(memory_space=pltpu.SMEM), vmem, pl.BlockSpec(memory_space=pl.ANY)] + [vmem] * len(terms)
    return whole_call(kernel, shapes, fetched(weight, blocks, width), MOST_VMEM, (cols, gated, weight, *terms), specs)


def shift(value, axis, by):
    size = lax.axis_size(axis)
    return lax.ppermute(value, axis, [(i, (i + by) % size) for i in range(size)])


def entering_states(state, rate, tokens):
    enter, total = jnp.zeros_like(state), state
    offset, span = jnp.int32(0), 1
    for axis in reversed(SEQ):
        size, index = lax.axis_size(axis), lax.axis_index(axis)
        if size == 2:
            other = lax.ppermute(total, axis, [(0, 1), (1, 0)])
            totals = [jnp.where(index == 0, total, other), jnp.where(index == 0, other, total)]
        else:
            copies = jnp.broadcast_to(total, (size, *total.shape))
            totals = lax.all_to_all(copies, axis, 0, 0, tiled=True)
        fade, before, total = jnp.exp(-rate * float(span * tokens)), jnp.zeros_like(state), jnp.zeros_like(state)
        for block in range(size):
            before = jnp.where(block == index, total, before)
            total = total * fade + totals[block]
        enter = enter + jnp.exp(-rate * (offset * tokens).astype(F32)) * before
        offset, span = offset + index * span, span * size
    return enter


def per_device(queries, key_proj, value_proj, decay_rate, residues, skip_gain, out_weight):
    tokens, chans = queries.shape
    modes = decay_rate.shape[1]
    seq_size = 1
    for axis in SEQ:
        seq_size *= lax.axis_size(axis)
    small = jax.ShapeDtypeStruct((modes, chans), F32)
    stacked = jax.ShapeDtypeStruct((tokens * chans // LANES, LANES), F32)
    args = (key_proj, value_proj, decay_rate.T, residues.T)
    ends = jax.ShapeDtypeStruct((modes, SUBS, chans), F32)
    rate, coef, ends, state, mixed = whole_call(
        functools.partial(state_kernel, float(tokens * seq_size)),
        (small, small, ends, small, stacked),
        [pltpu.VMEM(a.shape, a.dtype) for a in args] + [pltpu.SemaphoreType.DMA((len(args),))],
        ALL_VMEM,
        args,
        [pl.BlockSpec(memory_space=pl.ANY)] * len(args),
    )
    scratch = [pltpu.VMEM(stacked.shape, F32)]
    local = whole_call(local_kernel, stacked, scratch, ALL_VMEM, (mixed, rate, coef, ends, skip_gain[None, :]))
    enter = entering_states(state, rate, tokens)
    x_size, x_index = lax.axis_size("x"), lax.axis_index("x")
    z_size, z_index = lax.axis_size("zh"), lax.axis_index("zh").astype(jnp.int32)
    features = out_weight.shape[1] // (x_size * z_size)

    def cols(x_bys, chunk, first=jnp.int32(0)):
        lanes = []
        for x_by in x_bys:
            start = ((x_index + x_by) % x_size) * z_size
            lanes += [(start + z) * features + sum(WIDTHS[:chunk]) for z in (first, 1 - first)]
        return (jnp.stack(lanes) // LANES).astype(jnp.int32)

    def pair(chunk):
        return jax.ShapeDtypeStruct((2, tokens, WIDTHS[chunk]), F32)

    vmem, anywhere = pl.BlockSpec(memory_space=pltpu.VMEM), pl.BlockSpec(memory_space=pl.ANY)
    gated, far, near = whole_call(
        gate_kernel,
        (jax.ShapeDtypeStruct((tokens, chans), queries.dtype), pair(0), pair(0)),
        scratch + fetched(out_weight, 4, WIDTHS[0]),
        GATE_VMEM,
        (cols((2, -1), 0), queries, local, rate, coef, enter, out_weight),
        [pl.BlockSpec(memory_space=pltpu.SMEM)] + [vmem] * 5 + [anywhere],
    )
    ways = [1 if chunk % 2 == 0 else -1 for chunk in range(len(WIDTHS))]
    firsts = []
    for chunk, way in enumerate(ways):
        if chunk:
            kernel = functools.partial(project_kernel, 2)
            at = cols((2, -way), chunk)
            far, near = project_call(
                kernel, (pair(chunk), pair(chunk)), 4, WIDTHS[chunk], at, gated, out_weight, ()
            )
        firsts.append((shift(far, "x", way), near))
    seconds = []
    for chunk, way in enumerate(ways):
        passed, near = firsts[chunk]
        kernel = functools.partial(project_kernel, 1)
        (both,) = project_call(
            kernel, (pair(chunk),), 2, WIDTHS[chunk], cols((way,), chunk), gated, out_weight, (passed,)
        )
        seconds.append((shift(both, "x", way), shift(near, "x", -way)))
    outs = []
    for chunk, terms in enumerate(seconds):
        at = jnp.concatenate([cols((0,), chunk, z_index), z_index[None]])
        block = jax.ShapeDtypeStruct((tokens, WIDTHS[chunk]), F32)
        keep, send = project_call(own_kernel, (block, block), 2, WIDTHS[chunk], at, gated, out_weight, terms)
        outs.append(keep + shift(send, "zh", 1))
    return jnp.concatenate(outs, axis=1).astype(jnp.bfloat16)


def solution(mesh):
    sizes = [size for _, size in SEQ_PARTS + CHAN_PARTS]
    parts = Mesh(mesh.devices.reshape(sizes), SEQ + CHAN)
    in_specs = (
        P(SEQ, CHAN),
        P(SEQ, CHAN),
        P(SEQ, CHAN),
        P(CHAN, None),
        P(CHAN, None),
        P(CHAN),
        P(CHAN, None),
    )
    return jax.shard_map(
        per_device, mesh=parts, in_specs=in_specs, out_specs=P(SEQ, CHAN), check_vma=False
    )
```
